32 devices in a mesh: groups: 2 (over y), adapter: 4 (over z), tensor: 4 (over x, core).
Axes of the slice: x: 2, y: 2, z: 4, core: 2. Of those that a mesh axis runs over, the one named last changes fastest.
Arguments:
- tokens: bfloat16 [6144, 8192], P(('groups', 'adapter'), 'tensor'), parts along dimension 0, may hold values from -6 to 6
- token_adapter_index: int32 [6144, 1], P(('groups', 'adapter')), parts along dimension 0, may hold values from 0 to 15; in each aligned block of 768 rows (0 to 767, 768 to 1535, ...) at most 96 rows name the same one
- adapter_page_index: int32 [16], replicated, may hold values from 0 to 15, each once
- value_base_weight: bfloat16 [8192, 1024], P('tensor'), may hold values from -0.0625 to 0.0625
- adapter_down_weight: bfloat16 [16, 64, 8192], P('adapter', None, 'tensor'), may hold values from -0.0625 to 0.0625
- adapter_up_weight: bfloat16 [16, 64, 1024], P('adapter'), may hold values from -0.75 to 0.75
Outputs:
- values: bfloat16 [6144, 1024], P(('groups', 'adapter'), 'tensor'), parts along dimension 0
The draws below stay inside these ranges and needn't reach their ends.
There are 2 independent parts, one for each index of `groups`. The reference program is written for one: setup_inputs(seed, part) draws one part's arguments, and reference() takes and returns one part's arrays. A program takes and returns all parts, laid end to end along the dimension named above; an argument that names none is the same for every part. Nothing has to cross between parts.
Inputs may be any that keep to these rules, and one draw needn't show every extreme that they name: `token_adapter_index`: among the 768 tokens of one index of adapter (aligned blocks), no adapter is named by more than 96 tokens, a bound that some block reaches. Each page position belongs to exactly one adapter; adapter a's pages are row adapter_page_index[a] of adapter_down_weight and adapter_up_weight.
All inputs are finite; a program needn't handle non-finite values.
Results may differ from the reference program's by a relative error of at most 0.0042.
Values may be sent and summed in bfloat16 or wider, within the bound.
No kernel may reach another device: no remote copies, remote signals or barrier semaphores. Data moves between devices by JAX's collectives and lax.ppermute only.
A program may use at most 128 MiB of HBM per device.

```python
import math
import jax
import jax.numpy as jnp
import numpy as np
from jax import lax

MODEL_WIDTH = 8192
VALUE_WIDTH = 1024
ADAPTER_RANK = 64
TOK_DEV = 768
ADAPTER_COUNT = 16
CAP = 96
TOKENS = 3072
N_ADAPTER = 4
N_TENSOR = 4


def block_scale(key, dims, shards, least, largest):
    def one(dim, shards_of):
        steps = jax.random.uniform(jax.random.fold_in(jax.random.fold_in(key, 6), dim), (shards_of,), jnp.float32, least / len(shards), largest / len(shards))
        return jnp.repeat(jnp.exp(steps), dims[dim] // shards_of).reshape((-1,) + (1,) * (len(dims) - dim - 1))

    level = one(*shards[0])
    for cut in shards[1:]:
        level = level * one(*cut)
    return level


def deal_out(own_key, own, number, rows, amount, top, bound, lean):
    order = jax.random.permutation(own_key, amount)
    packed, ordinary = shares(amount, rows * top, bound, lean, True), shares(amount, rows * top, bound, lean, False)
    places = jnp.arange(amount)

    def named(tallies, rotation):
        used = int((tallies > 0).sum())
        fixed = max(1, used // 4)
        passed = fixed + (places - fixed + rotation * (used - fixed)) % max(1, amount - fixed)
        return jnp.zeros((amount,), jnp.int32).at[order[jnp.where(places < fixed, places, passed)]].set(jnp.asarray(tallies, jnp.int32))

    tallies = jnp.where(number % 4 == 0, named(packed, number // 4), named(ordinary, number - number // 4 - 1))
    mixed = jax.random.permutation(jax.random.fold_in(own, 3), amount)
    donor, sink = mixed[0:amount // 2 * 2:2], mixed[1:amount // 2 * 2:2]
    room = jnp.minimum(tallies[donor] - 1, bound - tallies[sink]) // 2
    room = jnp.where((donor == order[0]) | (sink == order[0]) | (tallies[sink] == 0), 0, jnp.maximum(room, 0))
    passed = jax.random.randint(jax.random.fold_in(own, 4), (amount // 2,), 0, 1 << 20) % (room + 1)
    tallies = tallies.at[donor].add(-passed).at[sink].add(passed)
    labels = jnp.searchsorted(jnp.cumsum(tallies), jnp.arange(rows * top), side="right").astype(jnp.int32)
    listing = labels.reshape(top, rows).T
    listing = listing[jax.random.permutation(jax.random.fold_in(own, 1), rows)]
    rotation = jax.random.randint(jax.random.fold_in(own, 2), (rows, 1), 0, top)
    return jnp.take_along_axis(listing, (jnp.arange(top)[None, :] + rotation) % top, axis=1)


def shares(number_of, total, most, lean, full):
    weights = [(1 << 20) // math.isqrt(grade ** lean) + 1 for grade in range(1, number_of + 1)]
    largest = most if full else min(most, max(-(-total // number_of), total * weights[0] // sum(weights)))
    least = 1 if total - largest >= number_of - 1 else 0
    holding, rest = [largest] + [least] * (number_of - 1), total - largest - least * (number_of - 1)
    while rest > 0:
        candidates = [i for i in range(1, number_of) if holding[i] < largest] or [i for i in range(1, number_of) if holding[i] < most]
        pool, left = sum([weights[i] for i in candidates]), rest
        for i in candidates:
            addition = min(most - holding[i], max(1, left * weights[i] // pool), rest)
            holding[i] = holding[i] + addition
            rest = rest - addition
    return np.array(holding)


def gaussian(own_key, dims, deviation, limit, pieces=(), kind=jnp.bfloat16):
    factor_of = block_scale(own_key, dims, pieces, -0.22, 0.18) if pieces else 1.0
    result = jax.random.normal(own_key, dims, jnp.float32) * deviation * factor_of
    return jnp.minimum(jnp.maximum(result, -limit), limit).astype(kind)


def setup_inputs(seed: int = 0, part: int = 0) -> dict:
    seeds = jax.random.split(jax.random.key(seed), 7)
    own_keys = jax.random.split(jax.random.fold_in(seeds[6], part), 7)
    tokens = gaussian(own_keys[0], (TOKENS, MODEL_WIDTH), 1.0, 6.0, ((0, 4), (1, 4)))
    token_adapter_index_keys = jax.random.split(jax.random.fold_in(own_keys[1], 1), TOKENS // TOK_DEV)
    token_adapter_index_turns = jax.random.permutation(jax.random.fold_in(own_keys[1], 3), TOKENS // TOK_DEV)
    token_adapter_index = jax.vmap(lambda own, number: deal_out(jax.random.fold_in(own_keys[1], 2), own, number, TOK_DEV, ADAPTER_COUNT, 1, CAP, 2))(token_adapter_index_keys, token_adapter_index_turns).reshape((TOKENS, 1))
    adapter_page_index = jax.random.permutation(seeds[2], ADAPTER_COUNT).astype(jnp.int32)
    value_base_weight = gaussian(seeds[3], (MODEL_WIDTH, VALUE_WIDTH), MODEL_WIDTH ** -0.5, 0.0625, ((0, 4),))
    adapter_down_weight = gaussian(seeds[4], (ADAPTER_COUNT, ADAPTER_RANK, MODEL_WIDTH), MODEL_WIDTH ** -0.5, 0.0625, ((0, 4), (2, 4)))
    adapter_up_weight = gaussian(seeds[5], (ADAPTER_COUNT, ADAPTER_RANK, VALUE_WIDTH), ADAPTER_RANK ** -0.5, 0.75, ((0, 4),))
    return {"tokens": tokens, "token_adapter_index": token_adapter_index, "adapter_page_index": adapter_page_index, "value_base_weight": value_base_weight, "adapter_down_weight": adapter_down_weight, "adapter_up_weight": adapter_up_weight}


def reference(tokens, token_adapter_index, adapter_page_index, value_base_weight, adapter_down_weight, adapter_up_weight):
    base = jnp.dot(tokens, value_base_weight, preferred_element_type=jnp.float32)
    chosen = token_adapter_index[:, 0].astype(jnp.int32)
    blocks = chosen.reshape(N_ADAPTER, TOK_DEV)
    onehot = (blocks[:, :, None] == jnp.arange(ADAPTER_COUNT, dtype=jnp.int32)[None, None, :]).astype(jnp.int32)
    position = jnp.sum(jnp.cumsum(onehot, axis=1) * onehot, axis=2) - 1
    source = jnp.arange(N_ADAPTER, dtype=jnp.int32)[:, None]
    span = N_ADAPTER * CAP
    target = (blocks * span + source * CAP + position).reshape(-1).astype(jnp.int32)
    slot_rows = jnp.zeros((ADAPTER_COUNT * span,), jnp.int32).at[target].set(jnp.arange(TOKENS, dtype=jnp.int32))
    slot_used = jnp.zeros((ADAPTER_COUNT * span,), jnp.int32).at[target].set(jnp.ones((TOKENS,), jnp.int32))
    slot_rows = slot_rows.reshape(ADAPTER_COUNT, span)
    slot_used = slot_used.reshape(ADAPTER_COUNT, span)
    share = MODEL_WIDTH // N_TENSOR

    def one_adapter(item):
        rows_idx, used, which = item
        rows = tokens[rows_idx] * used[:, None].astype(tokens.dtype)
        page_number = adapter_page_index[which]
        down_matrix_page = adapter_down_weight[page_number]
        up_matrix_page = adapter_up_weight[page_number]
        rows_split = rows.reshape(span, N_TENSOR, share).astype(jnp.float32)
        down_split = down_matrix_page.reshape(ADAPTER_RANK, N_TENSOR, share).astype(jnp.float32)
        shrink = jnp.einsum("tsf,rsf->tsr", rows_split, down_split, precision=lax.Precision.HIGHEST)
        shrink = shrink.astype(jnp.bfloat16).reshape(span, N_TENSOR * ADAPTER_RANK)
        up_tiled = jnp.tile(up_matrix_page, (N_TENSOR, 1))
        return jnp.dot(shrink, up_tiled, preferred_element_type=jnp.float32)

    deltas = lax.map(one_adapter, (slot_rows, slot_used, jnp.arange(ADAPTER_COUNT, dtype=jnp.int32)))
    delta = deltas.reshape(ADAPTER_COUNT * span, VALUE_WIDTH)[target]
    return (base + delta).astype(jnp.bfloat16)
```

```python
import jax
import jax.numpy as jnp
from jax import lax
from jax.sharding import PartitionSpec as P

F32 = jnp.float32
BF16 = jnp.bfloat16


def swap(x, axis, size, bit):
    return lax.ppermute(x, axis, [(i, i ^ bit) for i in range(size)])


def spread_over_holders(piece, axis, size):
    me = lax.axis_index(axis)
    if size == 4:
        near = swap(piece, axis, size, 1)
        far = swap(piece, axis, size, 2)
        middle = lax.ppermute(piece, axis, [(1, 2), (2, 1)])
        ends = lax.ppermute(far, axis, [(1, 0), (2, 3)])
        inner = (me == 1) | (me == 2)
        last = jnp.where(inner, middle, ends)
        return [(near, me ^ 1), (far, me ^ 2), (last, 3 - me)]
    found = []
    for step in range(1, size):
        piece = lax.ppermute(piece, axis, [(i, (i - 1) % size) for i in range(size)])
        found.append((piece, (me + step) % size))
    return found


def share_base(tokens, weight, axis, size):
    me = lax.axis_index(axis)
    block = weight.shape[1] // size
    if size & (size - 1):
        whole = jnp.dot(tokens, weight, preferred_element_type=F32)
        return lax.psum_scatter(whole, axis, scatter_dimension=1, tiled=True)

    def half(bit):
        columns = [lax.dynamic_slice_in_dim(weight, (2 * m + bit) * block, block, axis=1) for m in range(size // 2)]
        return jnp.dot(tokens, jnp.concatenate(columns, axis=1), preferred_element_type=F32)

    mine = me & 1
    held = half(mine) + swap(half(1 - mine), axis, size, 1)
    bit = 2
    while bit < size:
        mine = (me // bit) & 1
        count = held.shape[1] // block

        def pick(which):
            return jnp.concatenate(
                [lax.dynamic_slice_in_dim(held, (2 * m + which) * block, block, axis=1) for m in range(count // 2)],
                axis=1,
            )

        held = pick(mine) + swap(pick(1 - mine), axis, size, bit)
        bit *= 2
    return held


def make(sizes):
    groups, holders, tensor = sizes["groups"], sizes["adapter"], sizes["tensor"]

    def per_device(tokens, token_adapter_index, adapter_page_index, base_weight, down, up):
        rows, features = tokens.shape
        resident, rank, width = up.shape
        adapters = adapter_page_index.shape[0]
        block = width // tensor
        shared = groups if resident % groups == 0 else 1
        part = resident // shared
        group, holder, share = lax.axis_index("groups"), lax.axis_index("adapter"), lax.axis_index("tensor")

        chosen = token_adapter_index[:, 0]
        onehot = chosen[None, :] == jnp.arange(adapters, dtype=jnp.int32)[:, None]
        page = jnp.sum(jnp.where(onehot, adapter_page_index[:, None], 0), axis=0)

        up_mine = lax.dynamic_slice_in_dim(up.reshape(resident * rank, width), share * block, block, axis=1)
        own = jnp.concatenate([down.reshape(resident * rank, features), up_mine], axis=1)
        pieces = [(own, holder * resident)]
        mine = group if shared > 1 else 0
        sent = lax.dynamic_slice_in_dim(own, mine * part * rank, part * rank, axis=0)
        for piece, source in spread_over_holders(sent, "adapter", holders):
            pieces.append((piece, source * resident + mine * part))
            for step in range(1, shared):
                other = lax.ppermute(piece, "groups", [(i, (i + step) % shared) for i in range(shared)])
                pieces.append((other, source * resident + (group - step) % shared * part))

        base = share_base(tokens, base_weight, "tensor", tensor)

        shrink = jnp.zeros((rank, rows), F32)
        for piece, first in pieces:
            product = lax.dot_general(piece[:, :features], tokens, (((1,), (1,)), ((), ())), preferred_element_type=F32)
            for k in range(piece.shape[0] // rank):
                shrink = shrink + jnp.where(page[None, :] == first + k, product[k * rank : (k + 1) * rank], 0.0)
        shrink = shrink.astype(BF16)
        total = shrink.astype(F32)
        for step in range(1, tensor):
            other = lax.ppermute(shrink, "tensor", [(i, (i + step) % tensor) for i in range(tensor)])
            total = total + other.astype(F32)
        total = total.astype(BF16)

        ups = jnp.concatenate([piece[:, features:] for piece, _ in pieces], axis=0)
        spread = jnp.concatenate(
            [
                jnp.where(page[None, :] == first + k, total, 0)
                for piece, first in pieces
                for k in range(piece.shape[0] // rank)
            ],
            axis=0,
        )
        delta = lax.dot_general(spread, ups, (((0,), (0,)), ((), ())), preferred_element_type=F32)
        return (base + delta).astype(BF16)

    return per_device


def solution(mesh):
    placed = (
        P(("groups", "adapter"), "tensor"),
        P(("groups", "adapter"), None),
        P(),
        P("tensor", None),
        P("adapter", None, "tensor"),
        P("adapter", None, None),
    )
    return jax.shard_map(
        make(dict(mesh.shape)),
        mesh=mesh,
        in_specs=placed,
        out_specs=P(("groups", "adapter"), "tensor"),
        check_vma=False,
    )
```

```python
import functools

import jax
import jax.numpy as jnp
from jax import lax
from jax.experimental import pallas as pl
from jax.experimental.pallas import tpu as pltpu
from jax.sharding import PartitionSpec as P

F32 = jnp.float32
BF16 = jnp.bfloat16
MIB = 1024 * 1024
ANY = pl.BlockSpec(memory_space=pl.ANY)
VMEM = pl.BlockSpec(memory_space=pltpu.VMEM)
SMEM = pl.BlockSpec(memory_space=pltpu.SMEM)
DMA = pltpu.SemaphoreType.DMA


def swap(x, axis, size, bit):
    return lax.ppermute(x, axis, [(i, i ^ bit) for i in range(size)])


def shift(x, axis, size, step):
    return lax.ppermute(x, axis, [(i, (i + step) % size) for i in range(size)])


def row_tiles(rows):
    return 3 if rows % 384 == 0 else 1


def base_kernel(bits, tokens, weight, *refs):
    send, keep, held, slots, token_sems, weight_sems = refs[-6:]
    tiles, size = token_sems.shape[0], weight_sems.shape[0]
    half, block = size // 2, slots.shape[2]
    tile = tokens.shape[0] // tiles

    def fetch_tokens(t):
        part = pl.ds(t * tile, tile)
        return pltpu.make_async_copy(tokens.at[part], held.at[part], token_sems.at[t])

    def fetch_weight(m):
        which = bits[0] if m >= half else 1 - bits[0]
        column = pl.multiple_of((2 * (m % half) + which) * block, block)
        return pltpu.make_async_copy(weight.at[:, pl.ds(column, block)], slots.at[m], weight_sems.at[m])

    fetch_tokens(0).start()
    fetch_weight(0).start()
    for t in range(1, tiles):
        fetch_tokens(t).start()
    for m in range(1, size):
        fetch_weight(m).start()
    for m in range(size):
        fetch_weight(m).wait()
        to = keep if m >= half else send
        columns = slice(m % half * block, (m % half + 1) * block)
        for t in range(tiles):
            if m == 0:
                fetch_tokens(t).wait()
            part = slice(t * tile, (t + 1) * tile)
            to[part, columns] = jnp.dot(held[part, :], slots[m], preferred_element_type=F32).astype(to.dtype)


def base_halves(tokens, weight, bit, size, behind=()):
    rows, features = tokens.shape
    block = weight.shape[1] // size
    half = size // 2
    return pl.pallas_call(
        base_kernel,
        in_specs=[SMEM, ANY, ANY] + [ANY] * len(behind),
        out_specs=[VMEM, VMEM],
        out_shape=[jax.ShapeDtypeStruct((rows, half * block), BF16), jax.ShapeDtypeStruct((rows, half * block), F32)],
        scratch_shapes=[
            pltpu.VMEM((rows, features), tokens.dtype),
            pltpu.VMEM((size, features, block), weight.dtype),
            DMA((row_tiles(rows),)),
            DMA((size,)),
        ],
        compiler_params=pltpu.CompilerParams(vmem_limit_bytes=16 * MIB),
        cost_estimate=pl.CostEstimate(
            flops=2 * rows * features * block * size,
            bytes_accessed=2 * features * (rows + block * size),
            transcendentals=0,
        ),
    )(bit.reshape(1).astype(jnp.int32), tokens, weight, *behind)


def pass_kernel(flag, *refs):
    refs[-1][0] = flag[0]


def once(flag, *arrays):
    return pl.pallas_call(
        pass_kernel,
        in_specs=[SMEM] + [ANY] * len(arrays),
        out_specs=SMEM,
        out_shape=jax.ShapeDtypeStruct((1,), jnp.int32),
        compiler_params=pltpu.CompilerParams(vmem_limit_bytes=128 * 1024),
        cost_estimate=pl.CostEstimate(flops=0, bytes_accessed=0, transcendentals=0),
    )(flag.astype(jnp.int32).reshape(1), *arrays)


def make(sizes):
    groups, holders, tensor = sizes["groups"], sizes["adapter"], sizes["tensor"]

    def per_device(tokens, token_adapter_index, adapter_page_index, base_weight, down, up):
        rows, features = tokens.shape
        resident, rank, width = up.shape
        adapters = adapter_page_index.shape[0]
        block = width // tensor
        group, holder, share = lax.axis_index("groups"), lax.axis_index("adapter"), lax.axis_index("tensor")

        onehot = token_adapter_index[:, 0][None, :] == jnp.arange(adapters, dtype=jnp.int32)[:, None]
        page = jnp.sum(jnp.where(onehot, adapter_page_index[:, None], 0), axis=0)

        shared = groups if resident % groups == 0 else 1
        part = resident // shared
        mine = group if shared > 1 else 0
        piece = jnp.concatenate(
            [
                lax.dynamic_slice_in_dim(down, mine * part, part, axis=0).reshape(part * rank, features),
                lax.dynamic_slice(up, (mine * part, 0, share * block), (part, rank, block)).reshape(part * rank, block),
            ],
            axis=1,
        )
        own_up = lax.dynamic_slice_in_dim(up, share * block, block, axis=2).reshape(resident * rank, block)
        pieces = [(down.reshape(resident * rank, features), holder * resident)]
        line = holders == 4 and groups == 2 and tensor == 4
        if line and shared == 2:

            def ends(p):
                return lax.ppermute(p, "adapter", [(1, 0), (2, 3)])

            def middle(p):
                return lax.ppermute(p, "adapter", [(1, 2), (2, 1)])

            def across(p):
                return swap(p, "groups", 2, 1)

            def choose(flag, p, q):
                return jnp.where(flag.reshape(()) == 1, p, q)

            inner = ((holder == 1) | (holder == 2)).astype(jnp.int32)
            near = swap(piece, "adapter", 4, 1)
            mid = middle(piece)
            send, keep = base_halves(tokens, base_weight, share & 1, tensor)
            recv = swap(send, "tensor", tensor, 1)
            high = share // 2

            def pick(which):
                return lax.dynamic_slice_in_dim(keep, which * block, block, axis=1) + lax.dynamic_slice_in_dim(
                    recv, which * block, block, axis=1
                ).astype(F32)

            out, kept = pick(1 - high).astype(BF16), pick(high)
            other = swap(out, "tensor", tensor, 2)
            fout, fmid, ynear = ends(mid), middle(near), across(near)
            far = choose(once(inner, out), mid, fout)
            yfar = across(far)
            ready = once(inner, other, ynear)
            last = choose(ready, fmid, ends(fmid))
            lasts, ylasts = [last], [across(last)]
            base = kept + other.astype(F32)

            def add(source, these, those):
                for found, half in ((these, group), (those, 1 - group)):
                    first = source * resident + half * part
                    for p in found:
                        pieces.append((p, first))
                        first += p.shape[0] // rank

            add(holder ^ 1, [near], [ynear])
            add(jnp.where(inner == 1, holder ^ 3, holder ^ 2), [far], [yfar])
            add(jnp.where(inner == 1, holder ^ 2, holder ^ 3), lasts, ylasts)
        else:
            line = False
            whole = jnp.dot(tokens, base_weight, preferred_element_type=F32)
            base = lax.psum_scatter(whole, "tensor", scatter_dimension=1, tiled=True)
            for step in range(1, holders):
                piece = shift(piece, "adapter", holders, -1)
                source = (holder + step) % holders * resident
                pieces.append((piece, source + mine * part))
                for turn in range(1, shared):
                    pieces.append((shift(piece, "groups", groups, turn), source + (group - turn) % shared * part))

        shrink = jnp.zeros((rank, rows), F32)
        for piece, first in pieces:
            product = lax.dot_general(piece[:, :features], tokens, (((1,), (1,)), ((), ())), preferred_element_type=F32)
            for k in range(piece.shape[0] // rank):
                shrink = shrink + jnp.where(page[None, :] == first + k, product[k * rank : (k + 1) * rank], 0.0)
        shrink = shrink.astype(BF16)
        total = shrink.astype(F32)
        if line:
            total = total + swap(shrink, "tensor", tensor, 1).astype(F32)
            total = total + swap(total.astype(BF16), "tensor", tensor, 2).astype(F32)
        else:
            for step in range(1, tensor):
                total = total + shift(shrink, "tensor", tensor, step).astype(F32)
        total = total.astype(BF16)

        spread = jnp.concatenate(
            [
                jnp.where(page[None, :] == first + k, total, 0)
                for piece, first in pieces
                for k in range(piece.shape[0] // rank)
            ],
            axis=0,
        )
        ups = jnp.concatenate([own_up] + [piece[:, features:] for piece, _ in pieces[1:]], axis=0)
        delta = lax.dot_general(spread, ups, (((0,), (0,)), ((), ())), preferred_element_type=F32)
        return (base + delta).astype(BF16)

    return per_device


def solution(mesh):
    placed = (
        P(("groups", "adapter"), "tensor"),
        P(("groups", "adapter"), None),
        P(),
        P("tensor", None),
        P("adapter", None, "tensor"),
        P("adapter", None, None),
    )
    return jax.shard_map(
        make(dict(mesh.shape)),
        mesh=mesh,
        in_specs=placed,
        out_specs=P(("groups", "adapter"), "tensor"),
        check_vma=False,
    )
```

```python
import functools

import jax
import jax.numpy as jnp
from jax import lax
from jax.experimental import pallas as pl
from jax.experimental.pallas import tpu as pltpu
from jax.sharding import PartitionSpec as P

F32 = jnp.float32
MIB = 1024 * 1024
VMEM = pl.BlockSpec(memory_space=pltpu.VMEM)
DMA = pltpu.SemaphoreType.DMA
NO_COST = pl.CostEstimate(flops=0, bytes_accessed=0, transcendentals=0)
BF16 = jnp.bfloat16
ANY = pl.BlockSpec(memory_space=pl.ANY)
SMEM = pl.BlockSpec(memory_space=pltpu.SMEM)


def swap(x, axis, size, bit):
    return lax.ppermute(x, axis, [(i, i ^ bit) for i in range(size)])


def shift(x, axis, size, step):
    return lax.ppermute(x, axis, [(i, (i + step) % size) for i in range(size)])


def pass_kernel(flag, *refs):
    refs[-1][0] = flag[0]


def once(flag, *arrays):
    return pl.pallas_call(
        pass_kernel,
        in_specs=[SMEM] + [ANY] * len(arrays),
        out_specs=SMEM,
        out_shape=jax.ShapeDtypeStruct((1,), jnp.int32),
        compiler_params=pltpu.CompilerParams(vmem_limit_bytes=128 * 1024),
        cost_estimate=NO_COST,
    )(flag.astype(jnp.int32).reshape(1), *arrays)


def many_kernel(rank, count, numbers, page, tokens, *refs):
    pieces = refs[:count]
    acc, held, weights, token_sems, piece_sems = refs[-5:]
    before = refs[count] if len(refs) == count + 6 else None
    tiles = token_sems.shape[0]
    tile = tokens.shape[0] // tiles
    features = tokens.shape[1]

    def fetch_tokens(t):
        part = pl.ds(t * tile, tile)
        return pltpu.make_async_copy(tokens.at[part], held.at[part], token_sems.at[t])

    copies, named, first = [], [], 0
    for k, p in enumerate(pieces):
        here = pl.ds(first, p.shape[0])
        copies.append(pltpu.make_async_copy(p.at[:, pl.ds(0, features)], weights.at[here], piece_sems.at[k]))
        first += p.shape[0]
        named += [numbers[k] + j for j in range(p.shape[0] // rank)]
    fetch_tokens(0).start()
    for copy in copies:
        copy.start()
    for t in range(1, tiles):
        fetch_tokens(t).start()
    for copy in copies:
        copy.wait()
    chunk = 256 if weights.shape[0] % 256 == 0 else 128 if weights.shape[0] % 128 == 0 else weights.shape[0]
    for t in range(tiles):
        fetch_tokens(t).wait()
        part = slice(t * tile, (t + 1) * tile)
        pages = page[:, part]
        total = jnp.zeros((rank, tile), F32) if before is None else before[:, part]
        for c in range(0, weights.shape[0], chunk):
            product = lax.dot_general(
                weights[c : c + chunk, :], held[part, :], (((1,), (1,)), ((), ())), preferred_element_type=F32
            )
            for j in range(chunk // rank):
                mine = pages == named[c // rank + j]
                total = total + jnp.where(mine, product[j * rank : (j + 1) * rank], 0.0)
        acc[:, part] = total


def shrink_many(tokens, page, pieces, rank, before=None):
    rows, features = tokens.shape
    numbers = jnp.stack([first for _, first in pieces]).astype(jnp.int32)
    weights = [p for p, _ in pieces]
    tiles = 3 if rows % 384 == 0 else 1
    earlier = [] if before is None else [before]
    return pl.pallas_call(
        functools.partial(many_kernel, rank, len(weights)),
        in_specs=[SMEM, VMEM, ANY] + [ANY] * len(weights) + [VMEM] * len(earlier),
        out_specs=VMEM,
        out_shape=jax.ShapeDtypeStruct((rank, rows), F32),
        scratch_shapes=[
            pltpu.VMEM((rows, features), tokens.dtype),
            pltpu.VMEM((sum(w.shape[0] for w in weights), features), weights[0].dtype),
            DMA((tiles,)),
            DMA((len(weights),)),
        ],
        compiler_params=pltpu.CompilerParams(vmem_limit_bytes=12 * MIB),
        cost_estimate=NO_COST,
    )(numbers, page, tokens, *weights, *earlier)


def make(sizes):
    groups, holders, tensor = sizes["groups"], sizes["adapter"], sizes["tensor"]

    def per_device(tokens, token_adapter_index, adapter_page_index, base_weight, down, up):
        rows, features = tokens.shape
        resident, rank, width = up.shape
        adapters = adapter_page_index.shape[0]
        block = width // tensor
        group, holder, share = lax.axis_index("groups"), lax.axis_index("adapter"), lax.axis_index("tensor")

        onehot = token_adapter_index[:, 0][None, :] == jnp.arange(adapters, dtype=jnp.int32)[:, None]
        page = jnp.sum(jnp.where(onehot, adapter_page_index[:, None], 0), axis=0)

        shared = groups if resident % groups == 0 else 1
        part = resident // shared
        mine = group if shared > 1 else 0
        piece = jnp.concatenate(
            [
                lax.dynamic_slice_in_dim(down, mine * part, part, axis=0).reshape(part * rank, features),
                lax.dynamic_slice(up, (mine * part, 0, share * block), (part, rank, block)).reshape(part * rank, block),
            ],
            axis=1,
        )
        own_up = lax.dynamic_slice_in_dim(up, share * block, block, axis=2).reshape(resident * rank, block)
        pieces = [(down.reshape(resident * rank, features), holder * resident)]
        line = holders == 4 and groups == 2 and tensor == 4
        if line and shared == 2:

            def ends(p):
                return lax.ppermute(p, "adapter", [(1, 0), (2, 3)])

            def middle(p):
                return lax.ppermute(p, "adapter", [(1, 2), (2, 1)])

            def across(p):
                return swap(p, "groups", 2, 1)

            def choose(flag, p, q):
                return jnp.where(flag.reshape(()) == 1, p, q)

            inner = ((holder == 1) | (holder == 2)).astype(jnp.int32)
            near = swap(piece, "adapter", 4, 1)
            mid = middle(piece)
            whole = jnp.dot(tokens, base_weight, preferred_element_type=F32)
            low, high = share % 2, share // 2

            def columns(a, *starts):
                return jnp.concatenate([lax.dynamic_slice_in_dim(a, m * block, block, axis=1) for m in starts], axis=1)

            send = columns(whole, 1 - low, 3 - low).astype(BF16)
            recv = swap(send, "tensor", tensor, 1)

            def pick(which):
                return columns(whole, 2 * which + low) + columns(recv, which).astype(F32)

            out, kept = pick(1 - high).astype(BF16), pick(high)
            other = swap(out, "tensor", tensor, 2)
            fout, fmid, ynear = ends(mid), middle(near), across(near)
            far = choose(once(inner, out), mid, fout)
            yfar = across(far)
            def add(source, these, those):
                for found, half in ((these, group), (those, 1 - group)):
                    first = source * resident + half * part
                    for p in found:
                        pieces.append((p, first))
                        first += p.shape[0] // rank

            add(holder ^ 1, [near], [ynear])
            first_acc = shrink_many(tokens, page[None, :], pieces, rank)
            pieces_done = len(pieces)
            ready = once(inner, other)
            cut = part * rank // 2
            halves = lax.optimization_barrier((fmid[:cut], fmid[cut:]))
            lasts = [choose(ready, p, ends(p)) for p in halves]
            ylasts = [across(p) for p in lasts]
            base = kept + other.astype(F32)
            add(jnp.where(inner == 1, holder ^ 3, holder ^ 2), [far], [yfar])
            add(jnp.where(inner == 1, holder ^ 2, holder ^ 3), lasts, ylasts)
        else:
            line = False
            whole = jnp.dot(tokens, base_weight, preferred_element_type=F32)
            base = lax.psum_scatter(whole, "tensor", scatter_dimension=1, tiled=True)
            for step in range(1, holders):
                piece = shift(piece, "adapter", holders, -1)
                source = (holder + step) % holders * resident
                pieces.append((piece, source + mine * part))
                for turn in range(1, shared):
                    pieces.append((shift(piece, "groups", groups, turn), source + (group - turn) % shared * part))

        shrink, rest = jnp.zeros((rank, rows), F32), pieces
        if line:
            shrink = shrink_many(tokens, page[None, :], pieces[pieces_done:-2], rank, first_acc)
            rest = pieces[-2:]
        for piece, first in rest:
            product = lax.dot_general(piece[:, :features], tokens, (((1,), (1,)), ((), ())), preferred_element_type=F32)
            for k in range(piece.shape[0] // rank):
                shrink = shrink + jnp.where(page[None, :] == first + k, product[k * rank : (k + 1) * rank], 0.0)
        shrink = shrink.astype(BF16)
        total = shrink.astype(F32)
        if line:
            total = total + swap(shrink, "tensor", tensor, 1).astype(F32)
            total = total + swap(total.astype(BF16), "tensor", tensor, 2).astype(F32)
        else:
            for step in range(1, tensor):
                total = total + shift(shrink, "tensor", tensor, step).astype(F32)
        total = total.astype(BF16)

        spread = jnp.concatenate(
            [
                jnp.where(page[None, :] == first + k, total, 0)
                for piece, first in pieces
                for k in range(piece.shape[0] // rank)
            ],
            axis=0,
        )
        ups = jnp.concatenate([own_up] + [piece[:, features:] for piece, _ in pieces[1:]], axis=0)
        delta = lax.dot_general(spread, ups, (((0,), (0,)), ((), ())), preferred_element_type=F32)
        return (base + delta).astype(BF16)

    return per_device


def solution(mesh):
    placed = (
        P(("groups", "adapter"), "tensor"),
        P(("groups", "adapter"), None),
        P(),
        P("tensor", None),
        P("adapter", None, "tensor"),
        P("adapter", None, None),
    )
    return jax.shard_map(
        make(dict(mesh.shape)),
        mesh=mesh,
        in_specs=placed,
        out_specs=P(("groups", "adapter"), "tensor"),
        check_vma=False,
    )
```

```python
import functools

import jax
import jax.numpy as jnp
from jax import lax
from jax.experimental import pallas as pl
from jax.experimental.pallas import tpu as pltpu
from jax.sharding import PartitionSpec as P

F32 = jnp.float32
MIB = 1024 * 1024
VMEM = pl.BlockSpec(memory_space=pltpu.VMEM)
DMA = pltpu.SemaphoreType.DMA
NO_COST = pl.CostEstimate(flops=0, bytes_accessed=0, transcendentals=0)
BF16 = jnp.bfloat16
ANY = pl.BlockSpec(memory_space=pl.ANY)
SMEM = pl.BlockSpec(memory_space=pltpu.SMEM)


def swap(x, axis, size, bit):
    return lax.ppermute(x, axis, [(i, i ^ bit) for i in range(size)])


def shift(x, axis, size, step):
    return lax.ppermute(x, axis, [(i, (i + step) % size) for i in range(size)])


def pass_kernel(flag, *refs):
    refs[-1][0] = flag[0]


def once(flag, *arrays):
    return pl.pallas_call(
        pass_kernel,
        in_specs=[SMEM] + [ANY] * len(arrays),
        out_specs=SMEM,
        out_shape=jax.ShapeDtypeStruct((1,), jnp.int32),
        compiler_params=pltpu.CompilerParams(vmem_limit_bytes=128 * 1024),
        cost_estimate=NO_COST,
    )(flag.astype(jnp.int32).reshape(1), *arrays)


def many_kernel(rank, count, numbers, page, tokens, *refs):
    pieces = refs[:count]
    acc, held, weights, token_sems, piece_sems = refs[-5:]
    before = refs[count] if len(refs) == count + 6 else None
    tiles = token_sems.shape[0]
    tile = tokens.shape[0] // tiles
    features = tokens.shape[1]

    def fetch_tokens(t):
        part = pl.ds(t * tile, tile)
        return pltpu.make_async_copy(tokens.at[part], held.at[part], token_sems.at[t])

    copies, named, first = [], [], 0
    for k, p in enumerate(pieces):
        here = pl.ds(first, p.shape[0])
        copies.append(pltpu.make_async_copy(p.at[:, pl.ds(0, features)], weights.at[here], piece_sems.at[k]))
        first += p.shape[0]
        named += [numbers[k] + j for j in range(p.shape[0] // rank)]
    fetch_tokens(0).start()
    for copy in copies:
        copy.start()
    for t in range(1, tiles):
        fetch_tokens(t).start()
    for copy in copies:
        copy.wait()
    chunk = 256 if weights.shape[0] % 256 == 0 else 128 if weights.shape[0] % 128 == 0 else weights.shape[0]
    for t in range(tiles):
        fetch_tokens(t).wait()
        part = slice(t * tile, (t + 1) * tile)
        pages = page[:, part]
        total = jnp.zeros((rank, tile), F32) if before is None else before[:, part]
        for c in range(0, weights.shape[0], chunk):
            product = lax.dot_general(
                weights[c : c + chunk, :], held[part, :], (((1,), (1,)), ((), ())), preferred_element_type=F32
            )
            for j in range(chunk // rank):
                mine = pages == named[c // rank + j]
                total = total + jnp.where(mine, product[j * rank : (j + 1) * rank], 0.0)
        acc[:, part] = total


def shrink_many(tokens, page, pieces, rank, before=None):
    rows, features = tokens.shape
    numbers = jnp.stack([first for _, first in pieces]).astype(jnp.int32)
    weights = [p for p, _ in pieces]
    tiles = 3 if rows % 384 == 0 else 1
    earlier = [] if before is None else [before]
    return pl.pallas_call(
        functools.partial(many_kernel, rank, len(weights)),
        in_specs=[SMEM, VMEM, ANY] + [ANY] * len(weights) + [VMEM] * len(earlier),
        out_specs=VMEM,
        out_shape=jax.ShapeDtypeStruct((rank, rows), F32),
        scratch_shapes=[
            pltpu.VMEM((rows, features), tokens.dtype),
            pltpu.VMEM((sum(w.shape[0] for w in weights), features), weights[0].dtype),
            DMA((tiles,)),
            DMA((len(weights),)),
        ],
        compiler_params=pltpu.CompilerParams(vmem_limit_bytes=12 * MIB),
        cost_estimate=NO_COST,
    )(numbers, page, tokens, *weights, *earlier)


def last_kernel(total, other_total, page, names, ups, kept, other, out):
    rank, rows = total.shape
    tile = 256 if rows % 256 == 0 else rows
    for t in range(rows // tile):
        part = slice(t * tile, (t + 1) * tile)
        shrink = total[:, part] + other_total[:, part].astype(F32)
        pages = jnp.broadcast_to(page[:, part].astype(F32), (rank, tile))
        turned = jnp.concatenate([shrink, pages], axis=0).T
        shrink = turned[:, :rank]
        wide = jnp.concatenate([shrink] * (ups.shape[0] // rank), axis=1)
        spread = jnp.where(turned[:, rank : rank + 1] == names[...], wide, 0.0).astype(BF16)
        delta = jnp.dot(spread, ups[...], preferred_element_type=F32)
        out[part, :] = (delta + kept[part, :] + other[part, :].astype(F32)).astype(out.dtype)


def finish(total, other_total, page, names, ups, kept, other):
    rows, block = kept.shape
    return pl.pallas_call(
        last_kernel,
        in_specs=[VMEM] * 7,
        out_specs=VMEM,
        out_shape=jax.ShapeDtypeStruct((rows, block), BF16),
        compiler_params=pltpu.CompilerParams(vmem_limit_bytes=12 * MIB),
        cost_estimate=NO_COST,
    )(total, other_total, page, names, ups, kept, other)


def make(sizes):
    groups, holders, tensor = sizes["groups"], sizes["adapter"], sizes["tensor"]

    def per_device(tokens, token_adapter_index, adapter_page_index, base_weight, down, up):
        rows, features = tokens.shape
        resident, rank, width = up.shape
        adapters = adapter_page_index.shape[0]
        block = width // tensor
        group, holder, share = lax.axis_index("groups"), lax.axis_index("adapter"), lax.axis_index("tensor")

        onehot = token_adapter_index[:, 0][None, :] == jnp.arange(adapters, dtype=jnp.int32)[:, None]
        page = jnp.sum(jnp.where(onehot, adapter_page_index[:, None], 0), axis=0)

        shared = groups if resident % groups == 0 else 1
        part = resident // shared
        mine = group if shared > 1 else 0
        piece = jnp.concatenate(
            [
                lax.dynamic_slice_in_dim(down, mine * part, part, axis=0).reshape(part * rank, features),
                lax.dynamic_slice(up, (mine * part, 0, share * block), (part, rank, block)).reshape(part * rank, block),
            ],
            axis=1,
        )
        own_up = lax.dynamic_slice_in_dim(up, share * block, block, axis=2).reshape(resident * rank, block)
        pieces = [(down.reshape(resident * rank, features), holder * resident)]
        line = holders == 4 and groups == 2 and tensor == 4
        if line and shared == 2:

            def ends(p):
                return lax.ppermute(p, "adapter", [(1, 0), (2, 3)])

            def middle(p):
                return lax.ppermute(p, "adapter", [(1, 2), (2, 1)])

            def across(p):
                return swap(p, "groups", 2, 1)

            def choose(flag, p, q):
                return jnp.where(flag.reshape(()) == 1, p, q)

            inner = ((holder == 1) | (holder == 2)).astype(jnp.int32)
            near = swap(piece, "adapter", 4, 1)
            mid = middle(piece)
            whole = jnp.dot(tokens, base_weight, preferred_element_type=F32)
            low, high = share % 2, share // 2

            def columns(a, *starts):
                return jnp.concatenate([lax.dynamic_slice_in_dim(a, m * block, block, axis=1) for m in starts], axis=1)

            send = columns(whole, 1 - low, 3 - low).astype(BF16)
            recv = swap(send, "tensor", tensor, 1)

            def pick(which):
                return columns(whole, 2 * which + low) + columns(recv, which).astype(F32)

            out, kept = pick(1 - high).astype(BF16), pick(high)
            other = swap(out, "tensor", tensor, 2)
            fout, fmid, ynear = ends(mid), middle(near), across(near)
            far = choose(once(inner, out), mid, fout)
            yfar = across(far)
            def add(source, these, those):
                for found, half in ((these, group), (those, 1 - group)):
                    first = source * resident + half * part
                    for p in found:
                        pieces.append((p, first))
                        first += p.shape[0] // rank

            add(holder ^ 1, [near], [ynear])
            first_acc = shrink_many(tokens, page[None, :], pieces, rank)
            pieces_done = len(pieces)
            ready = once(inner, other)
            cut = part * rank // 2
            halves = lax.optimization_barrier((fmid[:cut], fmid[cut:]))
            lasts = [choose(ready, p, ends(p)) for p in halves]
            ylasts = [across(p) for p in lasts]
            add(jnp.where(inner == 1, holder ^ 3, holder ^ 2), [far], [yfar])
            add(jnp.where(inner == 1, holder ^ 2, holder ^ 3), lasts, ylasts)
        else:
            line = False
            whole = jnp.dot(tokens, base_weight, preferred_element_type=F32)
            base = lax.psum_scatter(whole, "tensor", scatter_dimension=1, tiled=True)
            for step in range(1, holders):
                piece = shift(piece, "adapter", holders, -1)
                source = (holder + step) % holders * resident
                pieces.append((piece, source + mine * part))
                for turn in range(1, shared):
                    pieces.append((shift(piece, "groups", groups, turn), source + (group - turn) % shared * part))

        shrink, rest = jnp.zeros((rank, rows), F32), pieces
        if line:
            shrink = shrink_many(tokens, page[None, :], pieces[pieces_done:-2], rank, first_acc)
            rest = pieces[-2:]
        for piece, first in rest:
            product = lax.dot_general(piece[:, :features], tokens, (((1,), (1,)), ((), ())), preferred_element_type=F32)
            for k in range(piece.shape[0] // rank):
                shrink = shrink + jnp.where(page[None, :] == first + k, product[k * rank : (k + 1) * rank], 0.0)
        shrink = shrink.astype(BF16)
        total = shrink.astype(F32)
        if line:
            total = total + swap(shrink, "tensor", tensor, 1).astype(F32)
            other_total = swap(total.astype(BF16), "tensor", tensor, 2)
        else:
            for step in range(1, tensor):
                total = total + shift(shrink, "tensor", tensor, step).astype(F32)

        ups = jnp.concatenate([own_up] + [piece[:, features:] for piece, _ in pieces[1:]], axis=0)
        if line:
            names = [first + k for piece, first in pieces for k in range(piece.shape[0] // rank)]
            names = jnp.repeat(jnp.stack(names).astype(F32), rank)[None, :]
            return finish(total, other_total, page[None, :], names, ups, kept, other)

        total = total.astype(BF16)
        spread = jnp.concatenate(
            [
                jnp.where(page[None, :] == first + k, total, 0)
                for piece, first in pieces
                for k in range(piece.shape[0] // rank)
            ],
            axis=0,
        )
        delta = lax.dot_general(spread, ups, (((0,), (0,)), ((), ())), preferred_element_type=F32)
        return (base + delta).astype(BF16)

    return per_device


def solution(mesh):
    placed = (
        P(("groups", "adapter"), "tensor"),
        P(("groups", "adapter"), None),
        P(),
        P("tensor", None),
        P("adapter", None, "tensor"),
        P("adapter", None, None),
    )
    return jax.shard_map(
        make(dict(mesh.shape)),
        mesh=mesh,
        in_specs=placed,
        out_specs=P(("groups", "adapter"), "tensor"),
        check_vma=False,
    )
```

```python
import functools

import jax
import jax.numpy as jnp
from jax import lax
from jax.experimental import pallas as pl
from jax.experimental.pallas import tpu as pltpu
from jax.sharding import PartitionSpec as P

F32 = jnp.float32
MIB = 1024 * 1024
VMEM = pl.BlockSpec(memory_space=pltpu.VMEM)
DMA = pltpu.SemaphoreType.DMA
NO_COST = pl.CostEstimate(flops=0, bytes_accessed=0, transcendentals=0)
BF16 = jnp.bfloat16
ANY = pl.BlockSpec(memory_space=pl.ANY)
SMEM = pl.BlockSpec(memory_space=pltpu.SMEM)


def swap(x, axis, size, bit):
    return lax.ppermute(x, axis, [(i, i ^ bit) for i in range(size)])


def shift(x, axis, size, step):
    return lax.ppermute(x, axis, [(i, (i + step) % size) for i in range(size)])


def pass_kernel(flag, *refs):
    refs[-1][0] = flag[0]


def once(flag, *arrays):
    return pl.pallas_call(
        pass_kernel,
        in_specs=[SMEM] + [ANY] * len(arrays),
        out_specs=SMEM,
        out_shape=jax.ShapeDtypeStruct((1,), jnp.int32),
        compiler_params=pltpu.CompilerParams(vmem_limit_bytes=128 * 1024),
        cost_estimate=NO_COST,
    )(flag.astype(jnp.int32).reshape(1), *arrays)


def many_kernel(rank, count, numbers, page, tokens, *refs):
    pieces = refs[:count]
    acc, held, weights, token_sems, piece_sems = refs[-5:]
    before = refs[count] if len(refs) == count + 6 else None
    tiles = token_sems.shape[0]
    tile = tokens.shape[0] // tiles
    features = tokens.shape[1]

    def fetch_tokens(t):
        part = pl.ds(t * tile, tile)
        return pltpu.make_async_copy(tokens.at[part], held.at[part], token_sems.at[t])

    copies, named, first = [], [], 0
    for k, p in enumerate(pieces):
        here = pl.ds(first, p.shape[0])
        copies.append(pltpu.make_async_copy(p.at[:, pl.ds(0, features)], weights.at[here], piece_sems.at[k]))
        first += p.shape[0]
        named += [numbers[k] + j for j in range(p.shape[0] // rank)]
    fetch_tokens(0).start()
    for copy in copies:
        copy.start()
    for t in range(1, tiles):
        fetch_tokens(t).start()
    for copy in copies:
        copy.wait()
    chunk = 256 if weights.shape[0] % 256 == 0 else 128 if weights.shape[0] % 128 == 0 else weights.shape[0]
    for t in range(tiles):
        fetch_tokens(t).wait()
        part = slice(t * tile, (t + 1) * tile)
        pages = page[:, part]
        total = jnp.zeros((rank, tile), F32) if before is None else before[:, part]
        for c in range(0, weights.shape[0], chunk):
            product = lax.dot_general(
                weights[c : c + chunk, :], held[part, :], (((1,), (1,)), ((), ())), preferred_element_type=F32
            )
            for j in range(chunk // rank):
                mine = pages == named[c // rank + j]
                total = total + jnp.where(mine, product[j * rank : (j + 1) * rank], 0.0)
        acc[:, part] = total


def shrink_many(tokens, page, pieces, rank, before=None):
    rows, features = tokens.shape
    numbers = jnp.stack([first for _, first in pieces]).astype(jnp.int32)
    weights = [p for p, _ in pieces]
    tiles = 3 if rows % 384 == 0 else 1
    earlier = [] if before is None else [before]
    return pl.pallas_call(
        functools.partial(many_kernel, rank, len(weights)),
        in_specs=[SMEM, VMEM, ANY] + [ANY] * len(weights) + [VMEM] * len(earlier),
        out_specs=VMEM,
        out_shape=jax.ShapeDtypeStruct((rank, rows), F32),
        scratch_shapes=[
            pltpu.VMEM((rows, features), tokens.dtype),
            pltpu.VMEM((sum(w.shape[0] for w in weights), features), weights[0].dtype),
            DMA((tiles,)),
            DMA((len(weights),)),
        ],
        compiler_params=pltpu.CompilerParams(vmem_limit_bytes=12 * MIB),
        cost_estimate=NO_COST,
    )(numbers, page, tokens, *weights, *earlier)


def last_kernel(total, other_total, page, names, ups, kept, other, out):
    rank, rows = total.shape
    tile = 256 if rows % 256 == 0 else rows
    for t in range(rows // tile):
        part = slice(t * tile, (t + 1) * tile)
        shrink = total[:, part] + other_total[:, part].astype(F32)
        pages = jnp.broadcast_to(page[:, part].astype(F32), (rank, tile))
        turned = jnp.concatenate([shrink, pages], axis=0).T
        shrink = turned[:, :rank]
        wide = jnp.concatenate([shrink] * (ups.shape[0] // rank), axis=1)
        spread = jnp.where(turned[:, rank : rank + 1] == names[...], wide, 0.0).astype(BF16)
        delta = jnp.dot(spread, ups[...], preferred_element_type=F32)
        out[part, :] = (delta + kept[part, :] + other[part, :].astype(F32)).astype(out.dtype)


def finish(total, other_total, page, names, ups, kept, other):
    rows, block = kept.shape
    return pl.pallas_call(
        last_kernel,
        in_specs=[VMEM] * 7,
        out_specs=VMEM,
        out_shape=jax.ShapeDtypeStruct((rows, block), BF16),
        compiler_params=pltpu.CompilerParams(vmem_limit_bytes=12 * MIB),
        cost_estimate=NO_COST,
    )(total, other_total, page, names, ups, kept, other)


def make(sizes):
    groups, holders, tensor = sizes["groups"], sizes["adapter"], sizes["tensor"]

    def per_device(tokens, token_adapter_index, adapter_page_index, base_weight, down, up):
        rows, features = tokens.shape
        resident, rank, width = up.shape
        adapters = adapter_page_index.shape[0]
        block = width // tensor
        group, holder, share = lax.axis_index("groups"), lax.axis_index("adapter"), lax.axis_index("tensor")

        onehot = token_adapter_index[:, 0][None, :] == jnp.arange(adapters, dtype=jnp.int32)[:, None]
        page = jnp.sum(jnp.where(onehot, adapter_page_index[:, None], 0), axis=0)

        shared = groups if resident % groups == 0 else 1
        part = resident // shared
        mine = group if shared > 1 else 0
        piece = jnp.concatenate(
            [
                lax.dynamic_slice_in_dim(down, mine * part, part, axis=0).reshape(part * rank, features),
                lax.dynamic_slice(up, (mine * part, 0, share * block), (part, rank, block)).reshape(part * rank, block),
            ],
            axis=1,
        )
        own_up = lax.dynamic_slice_in_dim(up, share * block, block, axis=2).reshape(resident * rank, block)
        pieces = [(down.reshape(resident * rank, features), holder * resident)]
        line = holders == 4 and groups == 2 and tensor == 4
        if line and shared == 2:

            def ends(p):
                return lax.ppermute(p, "adapter", [(1, 0), (2, 3)])

            def middle(p):
                return lax.ppermute(p, "adapter", [(1, 2), (2, 1)])

            def across(p):
                return swap(p, "groups", 2, 1)

            def choose(flag, p, q):
                return jnp.where(flag.reshape(()) == 1, p, q)

            inner = ((holder == 1) | (holder == 2)).astype(jnp.int32)
            near = swap(piece, "adapter", 4, 1)
            mid = middle(piece)
            whole = jnp.dot(tokens, base_weight, preferred_element_type=F32)
            low, high = share % 2, share // 2

            def columns(a, *starts):
                return jnp.concatenate([lax.dynamic_slice_in_dim(a, m * block, block, axis=1) for m in starts], axis=1)

            send = columns(whole, 1 - low, 3 - low).astype(BF16)
            recv = swap(send, "tensor", tensor, 1)

            def pick(which):
                return columns(whole, 2 * which + low) + columns(recv, which).astype(F32)

            out, kept = pick(1 - high).astype(BF16), pick(high)
            other = swap(out, "tensor", tensor, 2)
            fout, fmid, ynear = ends(mid), middle(near), across(near)
            far = choose(once(inner, out), mid, fout)
            yfar = across(far)
            def add(source, these, those):
                for found, half in ((these, group), (those, 1 - group)):
                    first = source * resident + half * part
                    for p in found:
                        pieces.append((p, first))
                        first += p.shape[0] // rank

            add(holder ^ 1, [near], [ynear])
            first_acc = shrink_many(tokens, page[None, :], pieces, rank)
            pieces_done = len(pieces)
            ready = once(inner, other)
            cut = part * rank // 2
            halves = lax.optimization_barrier((fmid[:cut], fmid[cut:]))
            lasts = [choose(ready, p, ends(p)) for p in halves]
            ylasts = [across(p) for p in lasts]
            add(jnp.where(inner == 1, holder ^ 3, holder ^ 2), [far], [yfar])
            add(jnp.where(inner == 1, holder ^ 2, holder ^ 3), lasts, ylasts)
        else:
            line = False
            whole = jnp.dot(tokens, base_weight, preferred_element_type=F32)
            base = lax.psum_scatter(whole, "tensor", scatter_dimension=1, tiled=True)
            for step in range(1, holders):
                piece = shift(piece, "adapter", holders, -1)
                source = (holder + step) % holders * resident
                pieces.append((piece, source + mine * part))
                for turn in range(1, shared):
                    pieces.append((shift(piece, "groups", groups, turn), source + (group - turn) % shared * part))

        shrink, rest = jnp.zeros((rank, rows), F32), pieces
        if line:
            shrink = shrink_many(tokens, page[None, :], pieces[pieces_done:-2], rank, first_acc)
            rest = pieces[-2:]
        for piece, first in rest:
            product = lax.dot_general(piece[:, :features], tokens, (((1,), (1,)), ((), ())), preferred_element_type=F32)
            for k in range(piece.shape[0] // rank):
                shrink = shrink + jnp.where(page[None, :] == first + k, product[k * rank : (k + 1) * rank], 0.0)
        shrink = shrink.astype(BF16)
        total = shrink.astype(F32)
        if line:
            total = total + swap(shrink, "tensor", tensor, 2).astype(F32)
            other_total = swap(total, "tensor", tensor, 1)
        else:
            for step in range(1, tensor):
                total = total + shift(shrink, "tensor", tensor, step).astype(F32)

        ups = jnp.concatenate([own_up] + [piece[:, features:] for piece, _ in pieces[1:]], axis=0)
        if line:
            names = [first + k for piece, first in pieces for k in range(piece.shape[0] // rank)]
            names = jnp.repeat(jnp.stack(names).astype(F32), rank)[None, :]
            return finish(total, other_total, page[None, :], names, ups, kept, other)

        total = total.astype(BF16)
        spread = jnp.concatenate(
            [
                jnp.where(page[None, :] == first + k, total, 0)
                for piece, first in pieces
                for k in range(piece.shape[0] // rank)
            ],
            axis=0,
        )
        delta = lax.dot_general(spread, ups, (((0,), (0,)), ((), ())), preferred_element_type=F32)
        return (base + delta).astype(BF16)

    return per_device


def solution(mesh):
    placed = (
        P(("groups", "adapter"), "tensor"),
        P(("groups", "adapter"), None),
        P(),
        P("tensor", None),
        P("adapter", None, "tensor"),
        P("adapter", None, None),
    )
    return jax.shard_map(
        make(dict(mesh.shape)),
        mesh=mesh,
        in_specs=placed,
        out_specs=P(("groups", "adapter"), "tensor"),
        check_vma=False,
    )
```
